32 devices in a mesh: parts: 2 (over x), brick: 16 (over z, y, core).
Axes of the slice: x: 2, y: 2, z: 4, core: 2. Of those that a mesh axis runs over, the one named last changes fastest.
Arguments:
- tokens: bfloat16 [4096, 1024], P(('parts', 'brick')), parts along dimension 0, may hold values from -6 to 6
- norm_gain: float32 [1024], replicated, may hold values from 0.5 to 2
- in_projection: bfloat16 [1024, 3072], replicated
- out_projection: bfloat16 [1024, 1024], replicated, may hold values from -0.1875 to 0.1875
- out_cotangent: bfloat16 [4096, 1024], P(('parts', 'brick')), parts along dimension 0, may hold values from -6 to 6
Outputs:
- layer_output: bfloat16 [4096, 1024], P(('parts', 'brick')), parts along dimension 0
- grad_tokens: bfloat16 [4096, 1024], P(('parts', 'brick')), parts along dimension 0
- grad_in_projection: float32 [2048, 3072], P(('parts', 'brick')), parts along dimension 0
- grad_out_projection: float32 [2048, 1024], P('parts', 'brick'), parts along dimension 0
- grad_norm_gain: float32 [2048], P(('parts', 'brick')), parts along dimension 0
The draws below stay inside these ranges and needn't reach their ends.
There are 2 independent parts, one for each index of `parts`. The reference program is written for one: setup_inputs(seed, part) draws one part's arguments, and reference() takes and returns one part's arrays. A program takes and returns all parts, laid end to end along the dimension named above; an argument that names none is the same for every part. Nothing has to cross between parts.
All inputs are finite; a program needn't handle non-finite values.
Results may differ from the reference program's by a relative error of at most 0.011.
Values may be sent and summed in bfloat16 or wider, within the bound.
A program may use at most 256 MiB of HBM per device.

```python
import math
import jax
import jax.numpy as jnp
from jax import lax

D = 1024
HEADS = 16
HEAD_DIM = 64
BRICK_A = 4
BRICK_B = 4
BRICK_C = 8
TOKENS = 2048
WINDOW = 256
N_BRICK = 16


def draw_in_projection(key, part):
    key = jax.random.fold_in(key, 17)
    first_key = jax.random.fold_in(key, 0)
    return (jax.random.normal(first_key, (D, 3 * D), jnp.float32) / math.sqrt(D)).astype(jnp.bfloat16)


def strengthened(entries, stream_key, source, target, shards_of, factor):
    def block_of(position):
        return (jnp.arange(entries.shape[position]) // (entries.shape[position] // shards_of)).reshape((-1,) + (1,) * (entries.ndim - 1 - position))

    first = jax.random.permutation(stream_key, shards_of)[block_of(target)]
    second = (block_of(target) + shards_of // 2) % shards_of
    return jnp.where((block_of(source) == first) | (block_of(source) == second), factor * entries, entries)


def level_of(stream_key, shape, shards, low, high):
    loudness = 1.0
    for dim, parts in shards:
        heights = jax.random.uniform(jax.random.fold_in(jax.random.fold_in(stream_key, 6), dim), (parts,), jnp.float32, low / len(shards), high / len(shards))
        loudness = loudness * jnp.repeat(jnp.exp(heights), shape[dim] // parts).reshape((-1,) + (1,) * (len(shape) - 1 - dim))
    return loudness


def scatter_about(stream_key, dims, spread, bound, cuts=(), kind=jnp.bfloat16):
    values = spread * jax.random.normal(stream_key, dims, jnp.float32)
    if cuts:
        values = values * level_of(stream_key, dims, cuts, -0.22, 0.18)
    return jnp.clip(values, -bound, bound).astype(kind)


def noise_with(rng, shape, scale, reach, pieces, heavy, dtype=jnp.bfloat16):
    drawn = scale * jax.random.normal(rng, shape, jnp.float32)
    if pieces:
        drawn = drawn * level_of(rng, shape, pieces, -0.22, 0.18)
    return jnp.clip(strengthened(drawn, jax.random.fold_in(rng, 3), *heavy), -reach, reach).astype(dtype)


def setup_inputs(seed: int = 0, part: int = 0) -> dict:
    keys = jax.random.split(jax.random.key(seed), 6)
    part_splits = jax.random.split(jax.random.fold_in(keys[5], part), 6)
    tokens = noise_with(part_splits[0], (TOKENS, D), 1.0, 6.0, ((0, 16),), (0, 1, 16, 2.0))
    norm_gain = jnp.clip(jnp.exp(jax.random.uniform(keys[1], (D,), jnp.float32, math.log(0.5), math.log(2.0))), 0.5, 2.0)
    in_projection = draw_in_projection(jax.random.fold_in(keys[5], 71), part)
    out_projection = scatter_about(keys[3], (D, D), D ** -0.5, 0.1875)
    out_cotangent = noise_with(part_splits[4], (TOKENS, D), 1.0, 6.0, ((0, 16),), (0, 1, 16, 2.0))
    return {"tokens": tokens, "norm_gain": norm_gain, "in_projection": in_projection, "out_projection": out_projection, "out_cotangent": out_cotangent}


norm_epsilon = 1e-05

def to_windows(values):
    width = values.shape[-1]
    shaped = values.reshape(N_BRICK, BRICK_A // 2, 2, BRICK_B // 2, 2, BRICK_C // 2, 2, width)
    return shaped.transpose(2, 4, 6, 0, 1, 3, 5, 7).reshape(8, TOKENS // 8, width)

def from_windows(values):
    width = values.shape[-1]
    shaped = values.reshape(2, 2, 2, N_BRICK, BRICK_A // 2, BRICK_B // 2, BRICK_C // 2, width)
    return shaped.transpose(3, 4, 0, 5, 1, 6, 2, 7).reshape(TOKENS, width)

def soft_of(queries, key_rows):
    score_scale = HEAD_DIM ** (-0.5)
    scores = jnp.dot(queries, key_rows.T, preferred_element_type=jnp.float32) * score_scale
    maxima = lax.optimization_barrier(jnp.max(scores, axis=-1, keepdims=True))
    shifted = jnp.exp(scores - maxima)
    totals = lax.optimization_barrier(jnp.sum(shifted, axis=-1, keepdims=True))
    return shifted / totals

def attend_item(triple):
    soft_weights = soft_of(triple[0], triple[1])
    soft_rounded = soft_weights.astype(jnp.bfloat16)
    return jnp.dot(soft_rounded, triple[2], preferred_element_type=jnp.float32).astype(jnp.bfloat16)

def attend_grad(inputs):
    triple, d_output = inputs
    queries, key_rows, value_rows = (triple[0], triple[1], triple[2])
    score_scale = HEAD_DIM ** (-0.5)
    soft_weights = soft_of(queries, key_rows)
    soft_rounded = soft_weights.astype(jnp.bfloat16)
    d_soft = jnp.dot(d_output, value_rows.T, preferred_element_type=jnp.float32)
    d_scores = soft_weights * (d_soft - lax.optimization_barrier(jnp.sum(soft_weights * d_soft, axis=-1, keepdims=True)))
    d_scaled = (d_scores * score_scale).astype(jnp.bfloat16)
    d_queries = jnp.dot(d_scaled, key_rows, preferred_element_type=jnp.float32).astype(jnp.bfloat16)
    d_keys = jnp.dot(d_scaled.T, queries, preferred_element_type=jnp.float32).astype(jnp.bfloat16)
    d_values = jnp.dot(soft_rounded.T, d_output, preferred_element_type=jnp.float32).astype(jnp.bfloat16)
    return jnp.stack([d_queries, d_keys, d_values])

def reference(tokens, norm_gain, in_projection, out_projection, out_cotangent):
    groups = TOKENS // 8 // WINDOW
    widened = tokens.astype(jnp.float32)
    centre = widened - lax.optimization_barrier(jnp.mean(widened, axis=-1, keepdims=True))
    inverse_dev = lax.rsqrt(lax.optimization_barrier(jnp.mean(centre * centre, axis=-1, keepdims=True)) + norm_epsilon)
    standard = centre * inverse_dev
    normed = (standard * norm_gain).astype(jnp.bfloat16)
    projected = jnp.dot(normed, in_projection, preferred_element_type=jnp.float32).astype(jnp.bfloat16)
    windows = to_windows(projected).reshape(8, groups, WINDOW, 3, HEADS, HEAD_DIM)
    item_stack = windows.transpose(0, 1, 4, 3, 2, 5).reshape(8 * groups * HEADS, 3, WINDOW, HEAD_DIM)
    attended_items = lax.map(attend_item, item_stack)
    attended_items = attended_items.reshape(8, groups, HEADS, WINDOW, HEAD_DIM).transpose(0, 1, 3, 2, 4)
    attended = from_windows(attended_items.reshape(8, TOKENS // 8, D))
    layer_output = jnp.dot(attended, out_projection, preferred_element_type=jnp.float32).astype(jnp.bfloat16)
    d_attended = jnp.dot(out_cotangent, out_projection.T, preferred_element_type=jnp.float32).astype(jnp.bfloat16)
    grad_out_projection = jnp.dot(attended.T, out_cotangent, preferred_element_type=jnp.float32)
    d_items = to_windows(d_attended).reshape(8, groups, WINDOW, HEADS, HEAD_DIM).transpose(0, 1, 3, 2, 4)
    d_items = d_items.reshape(8 * groups * HEADS, WINDOW, HEAD_DIM)
    item_grads = lax.map(attend_grad, (item_stack, d_items))
    d_windows = item_grads.reshape(8, groups, HEADS, 3, WINDOW, HEAD_DIM).transpose(0, 1, 4, 3, 2, 5)
    d_projected = from_windows(d_windows.reshape(8, TOKENS // 8, 3 * D))
    grad_in_projection = jnp.dot(normed.T, d_projected, preferred_element_type=jnp.float32)
    d_normed = jnp.dot(d_projected, in_projection.T, preferred_element_type=jnp.float32)
    grad_norm_gain = lax.optimization_barrier(jnp.sum(d_normed * standard, axis=0))
    weighted = d_normed * norm_gain
    mean_one = lax.optimization_barrier(jnp.mean(weighted, axis=-1, keepdims=True))
    mean_two = lax.optimization_barrier(jnp.mean(weighted * standard, axis=-1, keepdims=True))
    grad_tokens = (inverse_dev * (weighted - mean_one - standard * mean_two)).astype(jnp.bfloat16)
    return (layer_output, grad_tokens, grad_in_projection, grad_out_projection, grad_norm_gain)
```

```python
import functools

import jax
import jax.numpy as jnp
import numpy as np
from jax import lax
from jax.experimental import pallas as pl
from jax.experimental.pallas import tpu as pltpu
from jax.sharding import Mesh, PartitionSpec as P

D = 1024
HEADS = 16
HEAD_DIM = 64
GROUP = 16
CLASSES = 8
BLOCK = 16
HALF = 512
SCALE = HEAD_DIM ** (-0.5)
EPS = 1e-05
BF = jnp.bfloat16
F32 = jnp.float32
MESH = pl.DeviceIdType.MESH
MB = 1024 * 1024


def dot(a, b, ca, cb):
    return lax.dot_general(a, b, (((ca,), (cb,)), ((), ())), preferred_element_type=F32)


def permutation(transposed):
    shape = (128, 128)
    r = lax.broadcasted_iota(jnp.int32, shape, 1 if transposed else 0)
    s = lax.broadcasted_iota(jnp.int32, shape, 0 if transposed else 1)
    a = 2 * ((r >> 3) & 1) + ((r >> 6) & 1)
    p = 2 * ((r >> 2) & 1) + ((r >> 5) & 1)
    c = 2 * (r & 3) + ((r >> 4) & 1)
    return jnp.where(s == (a * 4 + p) * 8 + c, 1.0, 0.0).astype(BF)


def place():
    core = lax.axis_index("core")
    chip = lax.axis_index("chip")
    base = (chip // CLASSES) * CLASSES
    mine = (chip - base) * 2 + core
    return core, chip, base, mine


def device(base, local):
    return {"chip": base + local // 2, "core": local % 2}


def enter(base, mine):
    barrier = pltpu.get_barrier_semaphore()

    def greet(j, _):
        pl.semaphore_signal(
            barrier, inc=1, device_id=device(base, lax.rem(mine + j, GROUP)), device_id_type=MESH
        )
        return 0

    lax.fori_loop(1, GROUP, greet, 0)
    pl.semaphore_wait(barrier, GROUP - 1)


def gather_kernel(tok, cot, x, g, ptok, pcot, send, recv, psend, precv):
    core, chip, base, mine = place()
    perm = permutation(False)
    ptok[...] = jnp.dot(perm, tok[...], preferred_element_type=F32).astype(BF)
    pcot[...] = jnp.dot(perm, cot[...], preferred_element_type=F32).astype(BF)
    enter(base, mine)

    def copy(k, src, dst, peer, sender, j):
        rows = pl.ds(pl.multiple_of((peer // 2) * BLOCK, BLOCK), BLOCK)
        cols = pl.ds(pl.multiple_of((peer % 2) * HALF, HALF), HALF)
        landing = pl.ds(pl.multiple_of(sender * BLOCK, BLOCK), BLOCK)
        return pltpu.make_async_remote_copy(
            src_ref=src.at[rows, cols],
            dst_ref=dst.at[landing, cols],
            send_sem=send.at[k, j],
            recv_sem=recv.at[k, j],
            device_id=device(base, peer),
            device_id_type=MESH,
        )

    pairs = ((ptok, x), (pcot, g))
    for k, (src, dst) in enumerate(pairs):

        def start(j, _):
            copy(k, src, dst, lax.rem(mine + j, GROUP), mine, j).start()
            return 0

        lax.fori_loop(1, GROUP, start, 0)
    cols = pl.ds(pl.multiple_of(core * HALF, HALF), HALF)
    own = pl.ds(pl.multiple_of(mine * BLOCK, BLOCK), BLOCK)
    own_class = pl.ds(pl.multiple_of((mine // 2) * BLOCK, BLOCK), BLOCK)
    forwards = []
    for k, (src, dst) in enumerate(pairs):
        dst[own, cols] = src[own_class, cols]

        def finish(j, _):
            c = copy(k, src, dst, lax.rem(mine + j, GROUP), mine, j)
            c.wait_send()
            c.wait_recv()
            return 0

        lax.fori_loop(1, GROUP, finish, 0)
        f = pltpu.make_async_remote_copy(
            src_ref=dst.at[:, cols],
            dst_ref=dst.at[:, cols],
            send_sem=psend.at[k],
            recv_sem=precv.at[k],
            device_id={"core": 1 - core},
            device_id_type=MESH,
        )
        f.start()
        forwards.append(f)
    for f in forwards:
        f.wait_send()
        f.wait_recv()


def vmem():
    return pl.BlockSpec(memory_space=pltpu.VMEM)


def gather(tokens, cot):
    return pl.pallas_call(
        gather_kernel,
        out_shape=[jax.ShapeDtypeStruct((256, D), BF)] * 2,
        in_specs=[vmem()] * 2,
        out_specs=[vmem()] * 2,
        scratch_shapes=[
            pltpu.VMEM((128, D), BF),
            pltpu.VMEM((128, D), BF),
            pltpu.SemaphoreType.DMA((2, GROUP)),
            pltpu.SemaphoreType.DMA((2, GROUP)),
            pltpu.SemaphoreType.DMA((2,)),
            pltpu.SemaphoreType.DMA((2,)),
        ],
        compiler_params=pltpu.CompilerParams(
            collective_id=0, has_side_effects=True, vmem_limit_bytes=16 * MB
        ),
    )(tokens, cot)


def normalise(x):
    wide = x.astype(F32)
    centre = wide - jnp.mean(wide, axis=-1, keepdims=True)
    inverse = lax.rsqrt(jnp.mean(centre * centre, axis=-1, keepdims=True) + EPS)
    return centre * inverse, inverse


def work_kernel(x, g, gain, w_in, w_out, part_out, part_dn, terms, wi, wo, nrm, proj, att, dpr, sem):
    core = lax.axis_index("core")
    cols = pl.multiple_of(core * HALF, HALF)
    copies = [
        pltpu.make_async_copy(w_in.at[:, pl.ds(i * D + cols, HALF)], wi.at[i], sem.at[i])
        for i in range(3)
    ]
    copies.append(pltpu.make_async_copy(w_out.at[pl.ds(cols, HALF), :], wo, sem.at[3]))
    for c in copies:
        c.start()
    standard, _ = normalise(x[...])
    nrm[...] = (standard * gain[...]).astype(BF)
    for i in range(3):
        copies[i].wait()
        proj[i] = dot(nrm[...], wi[i], 1, 0).astype(BF)
    copies[3].wait()
    proj[3] = dot(g[...], wo[...], 1, 1).astype(BF)

    for h in range(HALF // HEAD_DIM):
        at = slice(h * HEAD_DIM, (h + 1) * HEAD_DIM)
        q, k, v, do = (proj[i, :, at] for i in range(4))
        scores = dot(q, k, 1, 1) * SCALE
        shifted = jnp.exp(scores - jnp.max(scores, axis=-1, keepdims=True))
        soft = shifted / jnp.sum(shifted, axis=-1, keepdims=True)
        rounded = soft.astype(BF)
        att[:, at] = dot(rounded, v, 1, 0).astype(BF)
        d_soft = dot(do, v, 1, 1)
        d_scores = soft * (d_soft - jnp.sum(soft * d_soft, axis=-1, keepdims=True))
        d_scaled = (d_scores * SCALE).astype(BF)
        dpr[0, :, at] = dot(d_scaled, k, 1, 0).astype(BF)
        dpr[1, :, at] = dot(d_scaled, q, 0, 0).astype(BF)
        dpr[2, :, at] = dot(rounded, do, 0, 0).astype(BF)

    part_out[...] = dot(att[...], wo[...], 1, 0)
    terms[:, 3 * HALF :] = dot(g[...], att[...], 0, 0).astype(BF)
    for i in range(3):
        terms[:, i * HALF : (i + 1) * HALF] = dot(nrm[...], dpr[i], 0, 0).astype(BF)
    part_dn[...] = (
        dot(dpr[0], wi[0], 1, 1) + dot(dpr[1], wi[1], 1, 1) + dot(dpr[2], wi[2], 1, 1)
    )


def work(x, g, gain, w_in, w_out):
    return pl.pallas_call(
        work_kernel,
        out_shape=[
            jax.ShapeDtypeStruct((256, D), F32),
            jax.ShapeDtypeStruct((256, D), F32),
            jax.ShapeDtypeStruct((D, 4 * HALF), BF),
        ],
        in_specs=[vmem()] * 3 + [pl.BlockSpec(memory_space=pl.ANY)] * 2,
        out_specs=[vmem()] * 3,
        scratch_shapes=[
            pltpu.VMEM((3, D, HALF), BF),
            pltpu.VMEM((HALF, D), BF),
            pltpu.VMEM((256, D), BF),
            pltpu.VMEM((4, 256, HALF), BF),
            pltpu.VMEM((256, HALF), BF),
            pltpu.VMEM((3, 256, HALF), BF),
            pltpu.SemaphoreType.DMA((4,)),
        ],
        compiler_params=pltpu.CompilerParams(vmem_limit_bytes=40 * MB),
    )(x, g, gain, w_in, w_out)


def return_kernel(x, gain, part_out, part_dn, out, grad, oland, dland, oret, dret, oin, din, psend, precv, send, recv):
    core, chip, base, mine = place()
    enter(base, mine)
    theirs = pl.ds(pl.multiple_of((1 - core) * 128, 128), 128)
    ours = pl.ds(pl.multiple_of(core * 128, 128), 128)
    swaps = []
    for k, (src, dst) in enumerate(((part_out, oland), (part_dn, dland))):
        c = pltpu.make_async_remote_copy(
            src_ref=src.at[theirs, :],
            dst_ref=dst,
            send_sem=psend.at[k],
            recv_sem=precv.at[k],
            device_id={"core": 1 - core},
            device_id_type=MESH,
        )
        c.start()
        swaps.append(c)

    def send_back(k, src, dst, j):
        brick = core * 8 + j
        rows = pl.ds(pl.multiple_of(j * BLOCK, BLOCK), BLOCK)
        landing = pl.ds(pl.multiple_of((mine // 2) * BLOCK, BLOCK), BLOCK)
        return pltpu.make_async_remote_copy(
            src_ref=src.at[rows, :],
            dst_ref=dst.at[landing, :],
            send_sem=send.at[k, j],
            recv_sem=recv.at[k, mine // 2],
            device_id=device(base, brick),
            device_id_type=MESH,
        )

    def deliver(k, src, dst):
        own_rows = pl.ds(pl.multiple_of((mine // 2) * BLOCK, BLOCK), BLOCK)
        for j in range(8):
            brick = core * 8 + j

            @pl.when(brick != mine)
            def _():
                send_back(k, src, dst, j).start()

            @pl.when(brick == mine)
            def _():
                dst[own_rows, :] = src[j * BLOCK : (j + 1) * BLOCK, :]

    swaps[0].wait_send()
    swaps[0].wait_recv()
    oret[...] = (part_out[ours, :] + oland[...]).astype(BF)
    deliver(0, oret, oin)
    swaps[1].wait_send()
    swaps[1].wait_recv()
    standard, inverse = normalise(x[ours, :])
    weighted = (part_dn[ours, :] + dland[...]) * gain[...]
    mean_one = jnp.mean(weighted, axis=-1, keepdims=True)
    mean_two = jnp.mean(weighted * standard, axis=-1, keepdims=True)
    dret[...] = (inverse * (weighted - mean_one - standard * mean_two)).astype(BF)
    deliver(1, dret, din)
    home = mine // 8
    inverse_perm = permutation(True)
    for k, (src, dst, result) in enumerate(((oret, oin, out), (dret, din, grad))):
        for j in range(8):

            @pl.when(core * 8 + j != mine)
            def _():
                send_back(k, src, dst, j).wait_send()

            @pl.when(j * 2 + home != mine)
            def _():
                pltpu.make_async_remote_copy(
                    src_ref=src.at[j * BLOCK : (j + 1) * BLOCK, :],
                    dst_ref=dst.at[j * BLOCK : (j + 1) * BLOCK, :],
                    send_sem=send.at[k, j],
                    recv_sem=recv.at[k, j],
                    device_id={"core": 1 - core},
                    device_id_type=MESH,
                ).wait_recv()

        result[...] = jnp.dot(inverse_perm, dst[...], preferred_element_type=F32).astype(BF)


def give_back(x, gain, part_out, part_dn):
    return pl.pallas_call(
        return_kernel,
        out_shape=[jax.ShapeDtypeStruct((128, D), BF)] * 2,
        in_specs=[vmem()] * 4,
        out_specs=[vmem()] * 2,
        scratch_shapes=[
            pltpu.VMEM((128, D), F32),
            pltpu.VMEM((128, D), F32),
            pltpu.VMEM((128, D), BF),
            pltpu.VMEM((128, D), BF),
            pltpu.VMEM((128, D), BF),
            pltpu.VMEM((128, D), BF),
            pltpu.SemaphoreType.DMA((2,)),
            pltpu.SemaphoreType.DMA((2,)),
            pltpu.SemaphoreType.DMA((2, 8)),
            pltpu.SemaphoreType.DMA((2, 8)),
        ],
        compiler_params=pltpu.CompilerParams(
            collective_id=1, has_side_effects=True, vmem_limit_bytes=24 * MB
        ),
    )(x, gain, part_out, part_dn)


def per_device(tokens, norm_gain, in_projection, out_projection, out_cotangent):
    core = lax.axis_index("core")
    chip = lax.axis_index("chip")
    gain = norm_gain.reshape(1, D)
    x, g = gather(tokens, out_cotangent)
    part_out, part_dn, terms = work(x, g, gain, in_projection, out_projection)
    summed = lax.psum_scatter(terms, "chip", scatter_dimension=0, tiled=True)
    layer_output, grad_tokens = give_back(x, gain, part_out, part_dn)
    rows = summed.shape[0] // 2
    theirs = lax.dynamic_slice_in_dim(summed, (1 - core) * rows, rows, 0)
    ours = lax.dynamic_slice_in_dim(summed, core * rows, rows, 0).astype(F32)
    got = lax.ppermute(theirs, "core", [(0, 1), (1, 0)]).astype(F32)
    low = jnp.where(core == 0, ours, got)
    high = jnp.where(core == 0, got, ours)
    both = jnp.stack([low.reshape(rows, 4, HALF), high.reshape(rows, 4, HALF)], axis=2)
    both = both.reshape(rows, 4, D)
    grad_in = both[:, :3].reshape(rows, 3 * D)
    grad_out = both[:, 3].T
    start = (chip * 2 + core) * rows
    w_rows = lax.dynamic_slice_in_dim(in_projection, start, rows, 0).astype(F32)
    my_gain = lax.dynamic_slice_in_dim(norm_gain, start, rows, 0)
    grad_gain = jnp.sum(w_rows * grad_in, axis=-1) / my_gain
    return layer_output, grad_tokens, grad_in, grad_out, grad_gain


def solution(mesh):
    parts, bricks = mesh.devices.shape
    fine = Mesh(mesh.devices.reshape(parts, bricks // 2, 2), ("parts", "chip", "core"))
    every = ("parts", "chip", "core")
    placed = (P(every, None), P(), P(), P(), P(every, None))
    return jax.shard_map(
        per_device,
        mesh=fine,
        in_specs=placed,
        out_specs=(
            P(every, None),
            P(every, None),
            P(every, None),
            P("parts", ("chip", "core")),
            P(every),
        ),
        check_vma=False,
    )
```

```python
import functools

import jax
import jax.numpy as jnp
import numpy as np
from jax import lax
from jax.experimental import pallas as pl
from jax.experimental.pallas import tpu as pltpu
from jax.sharding import Mesh, PartitionSpec as P

D = 1024
HEADS = 16
HEAD_DIM = 64
GROUP = 16
CLASSES = 8
BLOCK = 16
HALF = 512
SCALE = HEAD_DIM ** (-0.5)
EPS = 1e-05
BF = jnp.bfloat16
F32 = jnp.float32
MESH = pl.DeviceIdType.MESH
MB = 1024 * 1024


def dot(a, b, ca, cb):
    return lax.dot_general(a, b, (((ca,), (cb,)), ((), ())), preferred_element_type=F32)


def permutation(transposed):
    shape = (128, 128)
    r = lax.broadcasted_iota(jnp.int32, shape, 1 if transposed else 0)
    s = lax.broadcasted_iota(jnp.int32, shape, 0 if transposed else 1)
    a = 2 * ((r >> 3) & 1) + ((r >> 6) & 1)
    p = 2 * ((r >> 2) & 1) + ((r >> 5) & 1)
    c = 2 * (r & 3) + ((r >> 4) & 1)
    return jnp.where(s == (a * 4 + p) * 8 + c, 1.0, 0.0).astype(BF)


def place():
    core = lax.axis_index("core")
    chip = lax.axis_index("chip")
    base = (chip // CLASSES) * CLASSES
    mine = (chip - base) * 2 + core
    return core, chip, base, mine


def device(base, local):
    return {"chip": base + local // 2, "core": local % 2}


def enter(base, mine, low, high):
    barrier = pltpu.get_barrier_semaphore()

    def greet(j, _):
        pl.semaphore_signal(
            barrier, inc=1, device_id=device(base, lax.rem(mine + j, GROUP)), device_id_type=MESH
        )
        return 0

    lax.fori_loop(1, GROUP, greet, 0)
    pl.semaphore_wait(barrier, GROUP - 1)
    if high > 1 and low * high > CLASSES:
        chip = lax.axis_index("chip")
        level = chip // low
        for step, there in ((low, level < high - 1), (-low, level > 0)):

            @pl.when(there)
            def _():
                pl.semaphore_signal(
                    barrier, inc=1, device_id={"chip": chip + step}, device_id_type=MESH
                )

        for there in (level < high - 1, level > 0):

            @pl.when(there)
            def _():
                pl.semaphore_wait(barrier, 1)


def normalise(x):
    wide = x.astype(F32)
    centre = wide - jnp.mean(wide, axis=-1, keepdims=True)
    inverse = lax.rsqrt(jnp.mean(centre * centre, axis=-1, keepdims=True) + EPS)
    return centre * inverse, inverse


def vmem():
    return pl.BlockSpec(memory_space=pltpu.VMEM)


def chunk_of(kind, h):
    return h // 4 if kind == 3 else 2 + 3 * (h // 4) + kind


def kernel(
    low, high, tok, cot, gain, w_in, w_out, out, grad, gin, gout, gsum,
    ptok, pcot, x, g, wi, wo, nrm, proj, softs, feat, allf, alld, terms, inbox, outbox,
    part_out, part_dn, oland, dland, oret, dret, oin, din, fin, fland,
    wsem, gsend, grecv, psend, precv, fsend, frecv, dsend, drecv, zsend, zrecv, bsend, brecv,
):
    rows = D // (low * high)
    core, chip, base, mine = place()
    level, side = chip // low, lax.rem(chip, low)
    cols = pl.multiple_of(core * HALF, HALF)
    weights = [
        pltpu.make_async_copy(w_in.at[:, pl.ds(i * D + cols, HALF)], wi.at[i], wsem.at[i])
        for i in range(3)
    ]
    weights.append(pltpu.make_async_copy(w_out.at[pl.ds(cols, HALF), :], wo, wsem.at[3]))
    for c in weights:
        c.start()
    perm = permutation(False)
    ptok[...] = jnp.dot(perm, tok[...], preferred_element_type=F32).astype(BF)
    pcot[...] = jnp.dot(perm, cot[...], preferred_element_type=F32).astype(BF)
    enter(base, mine, low, high)

    def class_copy(k, src, dst, j):
        peer = lax.rem(mine + j, GROUP)
        there = pl.ds(pl.multiple_of((peer // 2) * BLOCK, BLOCK), BLOCK)
        span = pl.ds(pl.multiple_of((peer % 2) * HALF, HALF), HALF)
        landing = pl.ds(pl.multiple_of(mine * BLOCK, BLOCK), BLOCK)
        return pltpu.make_async_remote_copy(
            src_ref=src.at[there, span],
            dst_ref=dst.at[landing, span],
            send_sem=gsend.at[k, j],
            recv_sem=grecv.at[k, j],
            device_id=device(base, peer),
            device_id_type=MESH,
        )

    def partner(src, dst, slot):
        return pltpu.make_async_remote_copy(
            src_ref=src,
            dst_ref=dst,
            send_sem=psend.at[slot],
            recv_sem=precv.at[slot],
            device_id={"core": 1 - core},
            device_id_type=MESH,
        )

    def wait(c):
        c.wait_send()
        c.wait_recv()

    span = pl.ds(cols, HALF)
    own = pl.ds(pl.multiple_of(mine * BLOCK, BLOCK), BLOCK)
    own_class = pl.ds(pl.multiple_of((mine // 2) * BLOCK, BLOCK), BLOCK)
    pairs = ((ptok, x), (pcot, g))
    for k, (src, dst) in enumerate(pairs):

        def begin(j, _):
            class_copy(k, src, dst, j).start()
            return 0

        lax.fori_loop(1, GROUP, begin, 0)
        dst[own, span] = src[own_class, span]

    def arrived(k):
        src, dst = pairs[k]

        def finish(j, _):
            wait(class_copy(k, src, dst, j))
            return 0

        lax.fori_loop(1, GROUP, finish, 0)
        f = partner(dst.at[:, span], dst.at[:, span], k)
        f.start()
        return f

    def side_feature(k, j):
        peer = lax.rem(side + j, low)
        return pltpu.make_async_remote_copy(
            src_ref=feat.at[k, :, peer],
            dst_ref=allf.at[k, side],
            send_sem=fsend.at[k, j],
            recv_sem=frecv.at[k, j],
            device_id={"chip": chip - side + peer},
            device_id_type=MESH,
        )

    def side_chunk(c, j):
        peer = lax.rem(side + j, low)
        return pltpu.make_async_remote_copy(
            src_ref=alld.at[side, c],
            dst_ref=alld.at[side, c],
            send_sem=dsend.at[c, j],
            recv_sem=drecv.at[c, j],
            device_id={"chip": chip - side + peer},
            device_id_type=MESH,
        )

    def share_feature(k, turned):
        feat[k] = turned.reshape(high, low, rows, 256)
        for j in range(1, low):
            side_feature(k, j).start()
        allf[k, side] = feat[k, :, side]

    def share_chunk(c):
        for j in range(1, low):
            side_chunk(c, j).start()

    wait(arrived(0))
    standard, _ = normalise(x[...])
    scaled = standard * gain[...]
    nrm[...] = scaled.astype(BF)
    share_feature(0, scaled.T.astype(BF))
    for i in range(3):
        weights[i].wait()
        proj[i] = dot(nrm[...], wi[i], 1, 0).astype(BF)
    forward_g = arrived(1)

    heads = HALF // HEAD_DIM
    at = [slice(h * HEAD_DIM, (h + 1) * HEAD_DIM) for h in range(heads)]
    within = [slice((h % 4) * HEAD_DIM, (h % 4 + 1) * HEAD_DIM) for h in range(heads)]
    for h in range(heads):
        scores = dot(proj[0, :, at[h]], proj[1, :, at[h]], 1, 1) * SCALE
        shifted = jnp.exp(scores - jnp.max(scores, axis=-1, keepdims=True))
        soft = shifted / jnp.sum(shifted, axis=-1, keepdims=True)
        softs[h] = soft
        alld[side, chunk_of(3, h), :, within[h]] = dot(
            soft.astype(BF), proj[2, :, at[h]], 1, 0
        ).astype(BF)
        if h % 4 == 3:
            share_chunk(chunk_of(3, h))
    weights[3].wait()
    part_out[...] = dot(alld[side, 0], wo[:256, :], 1, 0) + dot(alld[side, 1], wo[256:, :], 1, 0)
    theirs = pl.ds(pl.multiple_of((1 - core) * 128, 128), 128)
    ours = pl.ds(pl.multiple_of(core * 128, 128), 128)
    swap_out = partner(part_out.at[theirs, :], oland, 2)
    swap_out.start()
    wait(forward_g)
    share_feature(1, g[...].astype(F32).T.astype(BF))
    proj[3] = dot(g[...], wo[...], 1, 1).astype(BF)

    def send_back(k, src, dst, j):
        landing = pl.ds(pl.multiple_of((mine // 2) * BLOCK, BLOCK), BLOCK)
        return pltpu.make_async_remote_copy(
            src_ref=src.at[j * BLOCK : (j + 1) * BLOCK, :],
            dst_ref=dst.at[landing, :],
            send_sem=bsend.at[k, j],
            recv_sem=brecv.at[k, mine // 2],
            device_id=device(base, core * 8 + j),
            device_id_type=MESH,
        )

    def deliver(k, src, dst):
        for j in range(8):

            @pl.when(core * 8 + j != mine)
            def _():
                send_back(k, src, dst, j).start()

            @pl.when(core * 8 + j == mine)
            def _():
                dst[own_class, :] = src[j * BLOCK : (j + 1) * BLOCK, :]

    wait(swap_out)
    oret[...] = (part_out[ours, :] + oland[...]).astype(BF)
    deliver(0, oret, oin)

    def backward(h):
        q, k, v, do = (proj[i, :, at[h]] for i in range(4))
        soft = softs[h]
        d_soft = dot(do, v, 1, 1)
        d_scores = soft * (d_soft - jnp.sum(soft * d_soft, axis=-1, keepdims=True))
        d_scaled = (d_scores * SCALE).astype(BF)
        w = within[h]
        alld[side, chunk_of(0, h), :, w] = dot(d_scaled, k, 1, 0).astype(BF)
        alld[side, chunk_of(1, h), :, w] = dot(d_scaled, q, 0, 0).astype(BF)
        alld[side, chunk_of(2, h), :, w] = dot(soft.astype(BF), do, 0, 0).astype(BF)
        if h % 4 == 3:
            for i in range(3):
                share_chunk(chunk_of(i, h))

    def line(way, t, c):
        return pltpu.make_async_remote_copy(
            src_ref=outbox.at[way, t, c],
            dst_ref=inbox.at[way, t, c],
            send_sem=zsend.at[way, t, c],
            recv_sem=zrecv.at[way, t, c],
            device_id={"chip": lax.rem(chip + (low if way == 0 else low * (high - 1)), low * high)},
            device_id_type=MESH,
        )

    def term(c):
        kind = jnp.where(c < 2, 1, 0)
        total = None
        for j in range(1, low):
            side_chunk(c, j).wait_recv()
        for s in range(low):
            part = dot(allf[kind, s].reshape(high * rows, 256), alld[s, c], 1, 0)
            total = part if total is None else total + part
        terms[c] = total.reshape(high, rows, 256)

    def relay(way, c):
        for t in range(high - 1, 0, -1) if way == 0 else range(high - 1):
            ahead = level < t if way == 0 else level > t
            first = level == (0 if way == 0 else high - 1)

            @pl.when(ahead & first)
            def _():
                outbox[way, t, c] = terms[c, t].astype(BF)
                line(way, t, c).start()

            @pl.when(ahead & jnp.logical_not(first))
            def _():
                line(way, t, c).wait_recv()
                outbox[way, t, c] = (terms[c, t] + inbox[way, t, c].astype(F32)).astype(BF)
                line(way, t, c).start()

    chunks = 8

    def step(s, fresh):
        if fresh:
            term(s)
        for way, lag in ((0, level), (1, high - 1 - level)):
            c = s - lag

            @pl.when((c >= 0) & (c < chunks))
            def _():
                relay(way, c)

    for h in range(4):
        backward(h)
    for k in range(2):
        for j in range(1, low):
            side_feature(k, j).wait_recv()
    step(0, True)
    for h in range(4, 8):
        backward(h)
    step(1, True)
    total = None
    for i in range(3):
        for half in range(2):
            part = dot(alld[side, 2 + 3 * half + i], wi[i, :, half * 256 : (half + 1) * 256], 1, 1)
            total = part if total is None else total + part
    part_dn[...] = total
    swap_dn = partner(part_dn.at[theirs, :], dland, 3)
    swap_dn.start()
    step(2, True)
    wait(swap_dn)
    standard, inverse = normalise(x[ours, :])
    weighted = (part_dn[ours, :] + dland[...]) * gain[...]
    mean_one = jnp.mean(weighted, axis=-1, keepdims=True)
    mean_two = jnp.mean(weighted * standard, axis=-1, keepdims=True)
    dret[...] = (inverse * (weighted - mean_one - standard * mean_two)).astype(BF)
    deliver(1, dret, din)

    def fresh_step(s, _):
        step(s, True)
        return 0

    def late_step(s, _):
        step(s, False)
        return 0

    lax.fori_loop(3, chunks, fresh_step, 0)
    lax.fori_loop(chunks, chunks + high - 1, late_step, 0)

    home = mine // 8
    inverse_perm = permutation(True)
    for k, (src, dst, result) in enumerate(((oret, oin, out), (dret, din, grad))):
        for j in range(8):

            @pl.when(core * 8 + j != mine)
            def _():
                send_back(k, src, dst, j).wait_send()

            @pl.when(j * 2 + home != mine)
            def _():
                pltpu.make_async_remote_copy(
                    src_ref=src.at[j * BLOCK : (j + 1) * BLOCK, :],
                    dst_ref=dst.at[j * BLOCK : (j + 1) * BLOCK, :],
                    send_sem=bsend.at[k, j],
                    recv_sem=brecv.at[k, j],
                    device_id={"core": 1 - core},
                    device_id_type=MESH,
                ).wait_recv()

        result[...] = jnp.dot(inverse_perm, dst[...], preferred_element_type=F32).astype(BF)

    w_rows = pl.ds(pl.multiple_of(chip * rows, rows), rows)
    gain_sum = jnp.zeros((rows, 1), F32)
    for c in range(chunks):
        span = slice(c * 256, (c + 1) * 256)
        fin[:, span] = terms[c, level]
        for way, there in ((0, level > 0), (1, level < high - 1)):

            @pl.when(there)
            def _():
                line(way, level, c).wait_recv()
                fin[:, span] += inbox[way, level, c].astype(F32)

        if c >= 2:
            half, i = divmod(c - 2, 3)
            w = wi[i, w_rows, half * 256 : (half + 1) * 256].astype(F32)
            gain_sum = gain_sum + jnp.sum(w * fin[:, span], axis=-1, keepdims=True)
    fin[:, chunks * 256 :] = jnp.broadcast_to(gain_sum, (rows, 128))
    few = rows // 2
    their_rows = pl.ds(pl.multiple_of((1 - core) * few, few), few)
    our_rows = pl.ds(pl.multiple_of(core * few, few), few)
    swap_fin = partner(fin.at[their_rows, :], fland, 4)
    swap_fin.start()

    def place_rows(who, values):
        for c in range(chunks):
            piece = values(slice(c * 256, (c + 1) * 256))
            if c < 2:
                gout[pl.ds(pl.multiple_of(who * HALF + c * 256, 256), 256), :] = piece.T
            else:
                half, i = divmod(c - 2, 3)
                where = pl.ds(pl.multiple_of(i * D + who * HALF + half * 256, 256), 256)
                gin[:, where] = piece

    place_rows(core, lambda s: fin[our_rows, s])
    wait(swap_fin)
    place_rows(1 - core, lambda s: fland[:, s])
    gsum[...] = fin[our_rows, chunks * 256 :] + fland[:, chunks * 256 :]

    for k in range(2):
        for j in range(1, low):
            side_feature(k, j).wait_send()

    def drain(c, _):
        for j in range(1, low):
            side_chunk(c, j).wait_send()
        for t in range(high):
            for way in range(2):
                sent = level < t if way == 0 else level > t

                @pl.when(sent)
                def _():
                    line(way, t, c).wait_send()

        return 0

    lax.fori_loop(0, chunks, drain, 0)


def per_device(tokens, norm_gain, in_projection, out_projection, out_cotangent):
    chips = lax.axis_size("chip")
    low = 1
    while 4 * low * low <= chips:
        low *= 2
    high = chips // low
    rows = D // chips
    few = rows // 2
    sems = pltpu.SemaphoreType.DMA
    layer_output, grad_tokens, grad_in, grad_out, gain_sum = pl.pallas_call(
        functools.partial(kernel, low, high),
        out_shape=[
            jax.ShapeDtypeStruct((128, D), BF),
            jax.ShapeDtypeStruct((128, D), BF),
            jax.ShapeDtypeStruct((few, 3 * D), F32),
            jax.ShapeDtypeStruct((D, few), F32),
            jax.ShapeDtypeStruct((few, 128), F32),
        ],
        in_specs=[vmem()] * 3 + [pl.BlockSpec(memory_space=pl.ANY)] * 2,
        out_specs=[vmem()] * 5,
        scratch_shapes=[
            pltpu.VMEM((128, D), BF),
            pltpu.VMEM((128, D), BF),
            pltpu.VMEM((256, D), BF),
            pltpu.VMEM((256, D), BF),
            pltpu.VMEM((3, D, HALF), BF),
            pltpu.VMEM((HALF, D), BF),
            pltpu.VMEM((256, D), BF),
            pltpu.VMEM((4, 256, HALF), BF),
            pltpu.VMEM((8, 256, 256), F32),
            pltpu.VMEM((2, high, low, rows, 256), BF),
            pltpu.VMEM((2, low, high, rows, 256), BF),
            pltpu.VMEM((low, 8, 256, 256), BF),
            pltpu.VMEM((8, high, rows, 256), F32),
            pltpu.VMEM((2, high, 8, rows, 256), BF),
            pltpu.VMEM((2, high, 8, rows, 256), BF),
            pltpu.VMEM((256, D), F32),
            pltpu.VMEM((256, D), F32),
            pltpu.VMEM((128, D), F32),
            pltpu.VMEM((128, D), F32),
            pltpu.VMEM((128, D), BF),
            pltpu.VMEM((128, D), BF),
            pltpu.VMEM((128, D), BF),
            pltpu.VMEM((128, D), BF),
            pltpu.VMEM((rows, 8 * 256 + 128), F32),
            pltpu.VMEM((few, 8 * 256 + 128), F32),
            sems((4,)),
            sems((2, GROUP)),
            sems((2, GROUP)),
            sems((5,)),
            sems((5,)),
            sems((2, low)),
            sems((2, low)),
            sems((8, low)),
            sems((8, low)),
            sems((2, high, 8)),
            sems((2, high, 8)),
            sems((2, 8)),
            sems((2, 8)),
        ],
        compiler_params=pltpu.CompilerParams(
            collective_id=0, has_side_effects=True, vmem_limit_bytes=56 * MB
        ),
    )(tokens, out_cotangent, norm_gain.reshape(1, D), in_projection, out_projection)
    start = (lax.axis_index("chip") * 2 + lax.axis_index("core")) * few
    my_gain = lax.dynamic_slice_in_dim(norm_gain, start, few, 0)
    return layer_output, grad_tokens, grad_in, grad_out, gain_sum[:, 0] / my_gain


def solution(mesh):
    parts, bricks = mesh.devices.shape
    fine = Mesh(mesh.devices.reshape(parts, bricks // 2, 2), ("parts", "chip", "core"))
    every = ("parts", "chip", "core")
    placed = (P(every, None), P(), P(), P(), P(every, None))
    return jax.shard_map(
        per_device,
        mesh=fine,
        in_specs=placed,
        out_specs=(
            P(every, None),
            P(every, None),
            P(every, None),
            P("parts", ("chip", "core")),
            P(every),
        ),
        check_vma=False,
    )
```

```python
import functools

import jax
import jax.numpy as jnp
import numpy as np
from jax import lax
from jax.experimental import pallas as pl
from jax.experimental.pallas import tpu as pltpu
from jax.sharding import Mesh, PartitionSpec as P

D = 1024
HEADS = 16
HEAD_DIM = 64
GROUP = 16
CLASSES = 8
BLOCK = 16
HALF = 512
SCALE = HEAD_DIM ** (-0.5)
EPS = 1e-05
BF = jnp.bfloat16
F32 = jnp.float32
MESH = pl.DeviceIdType.MESH
MB = 1024 * 1024


def dot(a, b, ca, cb):
    return lax.dot_general(a, b, (((ca,), (cb,)), ((), ())), preferred_element_type=F32)


def permutation(transposed):
    shape = (128, 128)
    r = lax.broadcasted_iota(jnp.int32, shape, 1 if transposed else 0)
    s = lax.broadcasted_iota(jnp.int32, shape, 0 if transposed else 1)
    a = 2 * ((r >> 3) & 1) + ((r >> 6) & 1)
    p = 2 * ((r >> 2) & 1) + ((r >> 5) & 1)
    c = 2 * (r & 3) + ((r >> 4) & 1)
    return jnp.where(s == (a * 4 + p) * 8 + c, 1.0, 0.0).astype(BF)


def place():
    core = lax.axis_index("core")
    chip = lax.axis_index("chip")
    base = (chip // CLASSES) * CLASSES
    mine = (chip - base) * 2 + core
    return core, chip, base, mine


def device(base, local):
    return {"chip": base + local // 2, "core": local % 2}


def enter(base, mine, low, high):
    barrier = pltpu.get_barrier_semaphore()

    def greet(j, _):
        pl.semaphore_signal(
            barrier, inc=1, device_id=device(base, lax.rem(mine + j, GROUP)), device_id_type=MESH
        )
        return 0

    lax.fori_loop(1, GROUP, greet, 0)
    pl.semaphore_wait(barrier, GROUP - 1)
    if high > 1 and low * high > CLASSES:
        chip = lax.axis_index("chip")
        level = chip // low
        for step, there in ((low, level < high - 1), (-low, level > 0)):

            @pl.when(there)
            def _():
                pl.semaphore_signal(
                    barrier, inc=1, device_id={"chip": chip + step}, device_id_type=MESH
                )

        for there in (level < high - 1, level > 0):

            @pl.when(there)
            def _():
                pl.semaphore_wait(barrier, 1)


def normalise(x):
    wide = x.astype(F32)
    centre = wide - jnp.mean(wide, axis=-1, keepdims=True)
    inverse = lax.rsqrt(jnp.mean(centre * centre, axis=-1, keepdims=True) + EPS)
    return centre * inverse, inverse


def vmem():
    return pl.BlockSpec(memory_space=pltpu.VMEM)


def chunk_of(kind, h):
    return h // 4 if kind == 3 else 2 + 3 * (h // 4) + kind


def kernel(
    low, high, tok, cot, gain, w_in, w_out, out, grad, gin, gout, gsum,
    ptok, pcot, x, g, wi, wo, nrm, proj, softs, feat, allf, alld, terms, inbox, outbox,
    part_out, part_dn, oland, dland, oret, dret, oin, din, fin, fland,
    wsem, gsend, grecv, psend, precv, fsend, frecv, dsend, drecv, zsend, zrecv, bsend, brecv,
):
    rows = D // (low * high)
    core, chip, base, mine = place()
    level, side = chip // low, lax.rem(chip, low)
    cols = pl.multiple_of(core * HALF, HALF)
    weights = [
        pltpu.make_async_copy(w_in.at[:, pl.ds(i * D + cols, HALF)], wi.at[i], wsem.at[i])
        for i in range(3)
    ]
    weights.append(pltpu.make_async_copy(w_out.at[pl.ds(cols, HALF), :], wo, wsem.at[3]))
    for c in weights:
        c.start()
    perm = permutation(False)
    ptok[...] = jnp.dot(perm, tok[...], preferred_element_type=F32).astype(BF)
    pcot[...] = jnp.dot(perm, cot[...], preferred_element_type=F32).astype(BF)
    enter(base, mine, low, high)

    def class_copy(k, src, dst, j):
        peer = lax.rem(mine + j, GROUP)
        there = pl.ds(pl.multiple_of((peer // 2) * BLOCK, BLOCK), BLOCK)
        span = pl.ds(pl.multiple_of((peer % 2) * HALF, HALF), HALF)
        landing = pl.ds(pl.multiple_of(mine * BLOCK, BLOCK), BLOCK)
        return pltpu.make_async_remote_copy(
            src_ref=src.at[there, span],
            dst_ref=dst.at[landing, span],
            send_sem=gsend.at[k, j],
            recv_sem=grecv.at[k, j],
            device_id=device(base, peer),
            device_id_type=MESH,
        )

    def partner(src, dst, slot):
        return pltpu.make_async_remote_copy(
            src_ref=src,
            dst_ref=dst,
            send_sem=psend.at[slot],
            recv_sem=precv.at[slot],
            device_id={"core": 1 - core},
            device_id_type=MESH,
        )

    def wait(c):
        c.wait_send()
        c.wait_recv()

    span = pl.ds(cols, HALF)
    own = pl.ds(pl.multiple_of(mine * BLOCK, BLOCK), BLOCK)
    own_class = pl.ds(pl.multiple_of((mine // 2) * BLOCK, BLOCK), BLOCK)
    pairs = ((ptok, x), (pcot, g))
    for k, (src, dst) in enumerate(pairs):

        def begin(j, _):
            class_copy(k, src, dst, j).start()
            return 0

        lax.fori_loop(1, GROUP, begin, 0)
        dst[own, span] = src[own_class, span]

    def arrived(k):
        src, dst = pairs[k]

        def finish(j, _):
            wait(class_copy(k, src, dst, j))
            return 0

        lax.fori_loop(1, GROUP, finish, 0)
        f = partner(dst.at[:, span], dst.at[:, span], k)
        f.start()
        return f

    def side_feature(k, j):
        peer = lax.rem(side + j, low)
        return pltpu.make_async_remote_copy(
            src_ref=feat.at[k, :, peer],
            dst_ref=allf.at[k, side],
            send_sem=fsend.at[k, j],
            recv_sem=frecv.at[k, j],
            device_id={"chip": chip - side + peer},
            device_id_type=MESH,
        )

    def side_chunk(c, j):
        peer = lax.rem(side + j, low)
        return pltpu.make_async_remote_copy(
            src_ref=alld.at[side, c],
            dst_ref=alld.at[side, c],
            send_sem=dsend.at[c, j],
            recv_sem=drecv.at[c, j],
            device_id={"chip": chip - side + peer},
            device_id_type=MESH,
        )

    def share_feature(k, turned):
        feat[k] = turned.reshape(high, low, rows, 256)
        for j in range(1, low):
            side_feature(k, j).start()
        allf[k, side] = feat[k, :, side]

    def share_chunk(c):
        for j in range(1, low):
            side_chunk(c, j).start()

    wait(arrived(0))
    standard, _ = normalise(x[...])
    scaled = standard * gain[...]
    nrm[...] = scaled.astype(BF)
    share_feature(0, scaled.T.astype(BF))
    for i in range(3):
        weights[i].wait()
        proj[i] = dot(nrm[...], wi[i], 1, 0).astype(BF)
    forward_g = arrived(1)

    heads = HALF // HEAD_DIM
    at = [slice(h * HEAD_DIM, (h + 1) * HEAD_DIM) for h in range(heads)]
    within = [slice((h % 4) * HEAD_DIM, (h % 4 + 1) * HEAD_DIM) for h in range(heads)]
    for h in range(heads):
        scores = dot(proj[0, :, at[h]], proj[1, :, at[h]], 1, 1) * SCALE
        shifted = jnp.exp(scores - jnp.max(scores, axis=-1, keepdims=True))
        soft = shifted / jnp.sum(shifted, axis=-1, keepdims=True)
        softs[h] = soft
        alld[side, chunk_of(3, h), :, within[h]] = dot(
            soft.astype(BF), proj[2, :, at[h]], 1, 0
        ).astype(BF)
        if h % 4 == 3:
            share_chunk(chunk_of(3, h))
    weights[3].wait()
    part_out[...] = dot(alld[side, 0], wo[:256, :], 1, 0) + dot(alld[side, 1], wo[256:, :], 1, 0)
    theirs = pl.ds(pl.multiple_of((1 - core) * 128, 128), 128)
    ours = pl.ds(pl.multiple_of(core * 128, 128), 128)
    swap_out = partner(part_out.at[theirs, :], oland, 2)
    swap_out.start()
    wait(forward_g)
    share_feature(1, g[...].astype(F32).T.astype(BF))
    proj[3] = dot(g[...], wo[...], 1, 1).astype(BF)

    def send_back(k, src, dst, j):
        landing = pl.ds(pl.multiple_of((mine // 2) * BLOCK, BLOCK), BLOCK)
        return pltpu.make_async_remote_copy(
            src_ref=src.at[j * BLOCK : (j + 1) * BLOCK, :],
            dst_ref=dst.at[landing, :],
            send_sem=bsend.at[k, j],
            recv_sem=brecv.at[k, mine // 2],
            device_id=device(base, core * 8 + j),
            device_id_type=MESH,
        )

    def deliver(k, src, dst):
        for j in range(8):

            @pl.when(core * 8 + j != mine)
            def _():
                send_back(k, src, dst, j).start()

            @pl.when(core * 8 + j == mine)
            def _():
                dst[own_class, :] = src[j * BLOCK : (j + 1) * BLOCK, :]

    wait(swap_out)
    oret[...] = (part_out[ours, :] + oland[...]).astype(BF)
    deliver(0, oret, oin)

    def backward(h):
        q, k, v, do = (proj[i, :, at[h]] for i in range(4))
        soft = softs[h]
        d_soft = dot(do, v, 1, 1)
        d_scores = soft * (d_soft - jnp.sum(soft * d_soft, axis=-1, keepdims=True))
        d_scaled = (d_scores * SCALE).astype(BF)
        w = within[h]
        alld[side, chunk_of(0, h), :, w] = dot(d_scaled, k, 1, 0).astype(BF)
        alld[side, chunk_of(1, h), :, w] = dot(d_scaled, q, 0, 0).astype(BF)
        alld[side, chunk_of(2, h), :, w] = dot(soft.astype(BF), do, 0, 0).astype(BF)
        if h % 4 == 3:
            for i in range(3):
                share_chunk(chunk_of(i, h))

    def line(way, t, c):
        return pltpu.make_async_remote_copy(
            src_ref=outbox.at[way, t, c],
            dst_ref=inbox.at[way, t, c],
            send_sem=zsend.at[way, t, c],
            recv_sem=zrecv.at[way, t, c],
            device_id={"chip": lax.rem(chip + (low if way == 0 else low * (high - 1)), low * high)},
            device_id_type=MESH,
        )

    def term(c):
        kind = jnp.where(c < 2, 1, 0)
        total = None
        for j in range(1, low):
            side_chunk(c, j).wait_recv()
        for s in range(low):
            part = dot(allf[kind, s].reshape(high * rows, 256), alld[s, c], 1, 0)
            total = part if total is None else total + part
        terms[c] = total.reshape(high, rows, 256)

    def relay(way, c):
        for t in range(high - 1, 0, -1) if way == 0 else range(high - 1):
            ahead = level < t if way == 0 else level > t
            first = level == (0 if way == 0 else high - 1)

            @pl.when(ahead & first)
            def _():
                outbox[way, t, c] = terms[c, t].astype(BF)
                line(way, t, c).start()

            @pl.when(ahead & jnp.logical_not(first))
            def _():
                line(way, t, c).wait_recv()
                outbox[way, t, c] = (terms[c, t] + inbox[way, t, c].astype(F32)).astype(BF)
                line(way, t, c).start()

    chunks = 8

    def step(s, fresh):
        if fresh:
            term(s)
        for way, lag in ((0, level), (1, high - 1 - level)):
            c = s - lag

            @pl.when((c >= 0) & (c < chunks))
            def _():
                relay(way, c)

    for h in range(4):
        backward(h)
    for k in range(2):
        for j in range(1, low):
            side_feature(k, j).wait_recv()
    step(0, True)
    for h in range(4, 8):
        backward(h)
    step(1, True)
    total = None
    for i in range(3):
        for half in range(2):
            part = dot(alld[side, 2 + 3 * half + i], wi[i, :, half * 256 : (half + 1) * 256], 1, 1)
            total = part if total is None else total + part
    part_dn[...] = total
    swap_dn = partner(part_dn.at[theirs, :], dland, 3)
    swap_dn.start()
    step(2, True)
    wait(swap_dn)
    standard, inverse = normalise(x[ours, :])
    weighted = (part_dn[ours, :] + dland[...]) * gain[...]
    mean_one = jnp.mean(weighted, axis=-1, keepdims=True)
    mean_two = jnp.mean(weighted * standard, axis=-1, keepdims=True)
    dret[...] = (inverse * (weighted - mean_one - standard * mean_two)).astype(BF)
    deliver(1, dret, din)

    def fresh_step(s, _):
        step(s, True)
        return 0

    def late_step(s, _):
        step(s, False)
        return 0

    lax.fori_loop(3, chunks, fresh_step, 0)
    lax.fori_loop(chunks, chunks + high - 1, late_step, 0)

    home = mine // 8
    inverse_perm = permutation(True)
    for k, (src, dst, result) in enumerate(((oret, oin, out), (dret, din, grad))):
        for j in range(8):

            @pl.when(core * 8 + j != mine)
            def _():
                send_back(k, src, dst, j).wait_send()

            @pl.when(j * 2 + home != mine)
            def _():
                pltpu.make_async_remote_copy(
                    src_ref=src.at[j * BLOCK : (j + 1) * BLOCK, :],
                    dst_ref=dst.at[j * BLOCK : (j + 1) * BLOCK, :],
                    send_sem=bsend.at[k, j],
                    recv_sem=brecv.at[k, j],
                    device_id={"core": 1 - core},
                    device_id_type=MESH,
                ).wait_recv()

        result[...] = jnp.dot(inverse_perm, dst[...], preferred_element_type=F32).astype(BF)

    w_rows = pl.ds(pl.multiple_of(chip * rows, rows), rows)
    gain_sum = jnp.zeros((rows, 1), F32)
    for c in range(chunks):
        span = slice(c * 256, (c + 1) * 256)
        fin[:, span] = terms[c, level]
        for way, there in ((0, level > 0), (1, level < high - 1)):

            @pl.when(there)
            def _():
                line(way, level, c).wait_recv()
                fin[:, span] += inbox[way, level, c].astype(F32)

        if c >= 2:
            half, i = divmod(c - 2, 3)
            w = wi[i, w_rows, half * 256 : (half + 1) * 256].astype(F32)
            gain_sum = gain_sum + jnp.sum(w * fin[:, span], axis=-1, keepdims=True)
    lane = lax.broadcasted_iota(jnp.int32, (rows, D), 1)
    mine_lane = chip * rows + lax.broadcasted_iota(jnp.int32, (rows, D), 0)
    my_gain = jnp.sum(jnp.where(lane == mine_lane, gain[...], 0.0), axis=-1, keepdims=True)
    fin[:, chunks * 256 :] = jnp.broadcast_to(gain_sum / my_gain, (rows, 128))
    few = rows // 2
    their_rows = pl.ds(pl.multiple_of((1 - core) * few, few), few)
    our_rows = pl.ds(pl.multiple_of(core * few, few), few)
    swap_fin = partner(fin.at[their_rows, :], fland, 4)
    swap_fin.start()

    def place_rows(who, values):
        for c in range(chunks):
            piece = values(slice(c * 256, (c + 1) * 256))
            if c < 2:
                gout[:, pl.ds(pl.multiple_of(who * HALF + c * 256, 256), 256)] = piece
            else:
                half, i = divmod(c - 2, 3)
                where = pl.ds(pl.multiple_of(i * D + who * HALF + half * 256, 256), 256)
                gin[:, where] = piece

    place_rows(core, lambda s: fin[our_rows, s])
    wait(swap_fin)
    place_rows(1 - core, lambda s: fland[:, s])
    gsum[...] = (fin[our_rows, chunks * 256 :] + fland[:, chunks * 256 :]).T[:1, :]

    for k in range(2):
        for j in range(1, low):
            side_feature(k, j).wait_send()

    def drain(c, _):
        for j in range(1, low):
            side_chunk(c, j).wait_send()
        for t in range(high):
            for way in range(2):
                sent = level < t if way == 0 else level > t

                @pl.when(sent)
                def _():
                    line(way, t, c).wait_send()

        return 0

    lax.fori_loop(0, chunks, drain, 0)


def settle_kernel(*refs):
    sem = refs[-1]
    half = (len(refs) - 1) // 2
    copies = [pltpu.make_async_copy(refs[i], refs[half + i], sem.at[i]) for i in range(half)]
    for c in copies:
        c.start()
    for c in copies:
        c.wait()


def settle(*arrays):
    anywhere = [pl.BlockSpec(memory_space=pl.ANY)] * len(arrays)
    return pl.pallas_call(
        settle_kernel,
        out_shape=[jax.ShapeDtypeStruct(a.shape, a.dtype) for a in arrays],
        in_specs=anywhere,
        out_specs=anywhere,
        scratch_shapes=[pltpu.SemaphoreType.DMA((len(arrays),))],
        compiler_params=pltpu.CompilerParams(vmem_limit_bytes=56 * MB),
    )(*arrays)


def per_device(tokens, norm_gain, in_projection, out_projection, out_cotangent):
    chips = lax.axis_size("chip")
    low = 1
    while 4 * low * low <= chips:
        low *= 2
    high = chips // low
    rows = D // chips
    few = rows // 2
    sems = pltpu.SemaphoreType.DMA
    layer_output, grad_tokens, grad_in, grad_out, gain_sum = pl.pallas_call(
        functools.partial(kernel, low, high),
        out_shape=[
            jax.ShapeDtypeStruct((128, D), BF),
            jax.ShapeDtypeStruct((128, D), BF),
            jax.ShapeDtypeStruct((few, 3 * D), F32),
            jax.ShapeDtypeStruct((few, D), F32),
            jax.ShapeDtypeStruct((1, few), F32),
        ],
        in_specs=[vmem()] * 3 + [pl.BlockSpec(memory_space=pl.ANY)] * 2,
        out_specs=[vmem()] * 5,
        scratch_shapes=[
            pltpu.VMEM((128, D), BF),
            pltpu.VMEM((128, D), BF),
            pltpu.VMEM((256, D), BF),
            pltpu.VMEM((256, D), BF),
            pltpu.VMEM((3, D, HALF), BF),
            pltpu.VMEM((HALF, D), BF),
            pltpu.VMEM((256, D), BF),
            pltpu.VMEM((4, 256, HALF), BF),
            pltpu.VMEM((8, 256, 256), F32),
            pltpu.VMEM((2, high, low, rows, 256), BF),
            pltpu.VMEM((2, low, high, rows, 256), BF),
            pltpu.VMEM((low, 8, 256, 256), BF),
            pltpu.VMEM((8, high, rows, 256), F32),
            pltpu.VMEM((2, high, 8, rows, 256), BF),
            pltpu.VMEM((2, high, 8, rows, 256), BF),
            pltpu.VMEM((256, D), F32),
            pltpu.VMEM((256, D), F32),
            pltpu.VMEM((128, D), F32),
            pltpu.VMEM((128, D), F32),
            pltpu.VMEM((128, D), BF),
            pltpu.VMEM((128, D), BF),
            pltpu.VMEM((128, D), BF),
            pltpu.VMEM((128, D), BF),
            pltpu.VMEM((rows, 8 * 256 + 128), F32),
            pltpu.VMEM((few, 8 * 256 + 128), F32),
            sems((4,)),
            sems((2, GROUP)),
            sems((2, GROUP)),
            sems((5,)),
            sems((5,)),
            sems((2, low)),
            sems((2, low)),
            sems((8, low)),
            sems((8, low)),
            sems((2, high, 8)),
            sems((2, high, 8)),
            sems((2, 8)),
            sems((2, 8)),
        ],
        compiler_params=pltpu.CompilerParams(
            collective_id=0, has_side_effects=True, vmem_limit_bytes=56 * MB
        ),
    )(tokens, out_cotangent, norm_gain.reshape(1, D), in_projection, out_projection)
    settled = settle(layer_output, grad_tokens, grad_in, grad_out, gain_sum)
    return settled[0], settled[1], settled[2], settled[3].T, settled[4].reshape(few)


def solution(mesh):
    parts, bricks = mesh.devices.shape
    fine = Mesh(mesh.devices.reshape(parts, bricks // 2, 2), ("parts", "chip", "core"))
    every = ("parts", "chip", "core")
    placed = (P(every, None), P(), P(), P(), P(every, None))
    return jax.shard_map(
        per_device,
        mesh=fine,
        in_specs=placed,
        out_specs=(
            P(every, None),
            P(every, None),
            P(every, None),
            P("parts", ("chip", "core")),
            P(every),
        ),
        check_vma=False,
    )
```

```python
import functools

import jax
import jax.numpy as jnp
import numpy as np
from jax import lax
from jax.experimental import pallas as pl
from jax.experimental.pallas import tpu as pltpu
from jax.sharding import Mesh, PartitionSpec as P

D = 1024
HEADS = 16
HEAD_DIM = 64
GROUP = 16
CLASSES = 8
BLOCK = 16
HALF = 512
SCALE = HEAD_DIM ** (-0.5)
EPS = 1e-05
BF = jnp.bfloat16
F32 = jnp.float32
MESH = pl.DeviceIdType.MESH
MB = 1024 * 1024


def dot(a, b, ca, cb):
    return lax.dot_general(a, b, (((ca,), (cb,)), ((), ())), preferred_element_type=F32)


def permutation(transposed):
    shape = (128, 128)
    r = lax.broadcasted_iota(jnp.int32, shape, 1 if transposed else 0)
    s = lax.broadcasted_iota(jnp.int32, shape, 0 if transposed else 1)
    a = 2 * ((r >> 3) & 1) + ((r >> 6) & 1)
    p = 2 * ((r >> 2) & 1) + ((r >> 5) & 1)
    c = 2 * (r & 3) + ((r >> 4) & 1)
    return jnp.where(s == (a * 4 + p) * 8 + c, 1.0, 0.0).astype(BF)


def place():
    core = lax.axis_index("core")
    chip = lax.axis_index("chip")
    base = (chip // CLASSES) * CLASSES
    mine = (chip - base) * 2 + core
    return core, chip, base, mine


def device(base, local):
    return {"chip": base + local // 2, "core": local % 2}


def enter(base, mine, low, high):
    barrier = pltpu.get_barrier_semaphore()

    def greet(j, _):
        pl.semaphore_signal(
            barrier, inc=1, device_id=device(base, lax.rem(mine + j, GROUP)), device_id_type=MESH
        )
        return 0

    lax.fori_loop(1, GROUP, greet, 0)
    pl.semaphore_wait(barrier, GROUP - 1)
    if high > 1 and low * high > CLASSES:
        chip = lax.axis_index("chip")
        level = chip // low
        for step, there in ((low, level < high - 1), (-low, level > 0)):

            @pl.when(there)
            def _():
                pl.semaphore_signal(
                    barrier, inc=1, device_id={"chip": chip + step}, device_id_type=MESH
                )

        for there in (level < high - 1, level > 0):

            @pl.when(there)
            def _():
                pl.semaphore_wait(barrier, 1)


def normalise(x):
    wide = x.astype(F32)
    centre = wide - jnp.mean(wide, axis=-1, keepdims=True)
    inverse = lax.rsqrt(jnp.mean(centre * centre, axis=-1, keepdims=True) + EPS)
    return centre * inverse, inverse


def vmem():
    return pl.BlockSpec(memory_space=pltpu.VMEM)


def chunk_of(kind, h):
    return h // 4 if kind == 3 else 2 + 3 * (h // 4) + kind


def kernel(
    low, high, tok, cot, gain, w_in, w_out, out, grad, gin, gout, gsum,
    ptok, pcot, x, g, wi, wo, nrm, proj, softs, feat, allf, alld, terms, inbox, outbox,
    part_out, part_dn, oland, dland, oret, dret, oin, din, fin, fland,
    wsem, gsend, grecv, psend, precv, fsend, frecv, dsend, drecv, zsend, zrecv, bsend, brecv,
):
    rows = D // (low * high)
    core, chip, base, mine = place()
    level, side = chip // low, lax.rem(chip, low)
    cols = pl.multiple_of(core * HALF, HALF)
    weights = [
        pltpu.make_async_copy(w_in.at[:, pl.ds(i * D + cols, HALF)], wi.at[i], wsem.at[i])
        for i in range(3)
    ]
    weights.append(pltpu.make_async_copy(w_out.at[pl.ds(cols, HALF), :], wo, wsem.at[3]))
    for c in weights:
        c.start()
    perm = permutation(False)
    ptok[...] = jnp.dot(perm, tok[...], preferred_element_type=F32).astype(BF)
    pcot[...] = jnp.dot(perm, cot[...], preferred_element_type=F32).astype(BF)
    enter(base, mine, low, high)

    def class_copy(k, src, dst, j):
        peer = lax.rem(mine + j, GROUP)
        there = pl.ds(pl.multiple_of((peer // 2) * BLOCK, BLOCK), BLOCK)
        span = pl.ds(pl.multiple_of((peer % 2) * HALF, HALF), HALF)
        landing = pl.ds(pl.multiple_of(mine * BLOCK, BLOCK), BLOCK)
        return pltpu.make_async_remote_copy(
            src_ref=src.at[there, span],
            dst_ref=dst.at[landing, span],
            send_sem=gsend.at[k, j],
            recv_sem=grecv.at[k, j],
            device_id=device(base, peer),
            device_id_type=MESH,
        )

    def partner(src, dst, slot):
        return pltpu.make_async_remote_copy(
            src_ref=src,
            dst_ref=dst,
            send_sem=psend.at[slot],
            recv_sem=precv.at[slot],
            device_id={"core": 1 - core},
            device_id_type=MESH,
        )

    def wait(c):
        c.wait_send()
        c.wait_recv()

    span = pl.ds(cols, HALF)
    own = pl.ds(pl.multiple_of(mine * BLOCK, BLOCK), BLOCK)
    own_class = pl.ds(pl.multiple_of((mine // 2) * BLOCK, BLOCK), BLOCK)
    pairs = ((ptok, x), (pcot, g))
    for k, (src, dst) in enumerate(pairs):

        def begin(j, _):
            class_copy(k, src, dst, j).start()
            return 0

        lax.fori_loop(1, GROUP, begin, 0)
        dst[own, span] = src[own_class, span]

    def arrived(k):
        src, dst = pairs[k]

        def finish(j, _):
            wait(class_copy(k, src, dst, j))
            return 0

        lax.fori_loop(1, GROUP, finish, 0)
        f = partner(dst.at[:, span], dst.at[:, span], k)
        f.start()
        return f

    def side_feature(k, j):
        peer = lax.rem(side + j, low)
        return pltpu.make_async_remote_copy(
            src_ref=feat.at[k, :, peer],
            dst_ref=allf.at[k, side],
            send_sem=fsend.at[k, j],
            recv_sem=frecv.at[k, j],
            device_id={"chip": chip - side + peer},
            device_id_type=MESH,
        )

    def side_chunk(c, j):
        peer = lax.rem(side + j, low)
        return pltpu.make_async_remote_copy(
            src_ref=alld.at[side, c],
            dst_ref=alld.at[side, c],
            send_sem=dsend.at[c, j],
            recv_sem=drecv.at[c, j],
            device_id={"chip": chip - side + peer},
            device_id_type=MESH,
        )

    def share_feature(k, turned):
        feat[k] = turned.reshape(high, low, rows, 256)
        for j in range(1, low):
            side_feature(k, j).start()
        allf[k, side] = feat[k, :, side]

    def share_chunk(c):
        for j in range(1, low):
            side_chunk(c, j).start()

    wait(arrived(0))
    standard, _ = normalise(x[...])
    scaled = standard * gain[...]
    nrm[...] = scaled.astype(BF)
    share_feature(0, scaled.T.astype(BF))
    for i in range(3):
        weights[i].wait()
        proj[i] = dot(nrm[...], wi[i], 1, 0).astype(BF)
    forward_g = arrived(1)

    heads = HALF // HEAD_DIM
    at = [slice(h * HEAD_DIM, (h + 1) * HEAD_DIM) for h in range(heads)]
    within = [slice((h % 4) * HEAD_DIM, (h % 4 + 1) * HEAD_DIM) for h in range(heads)]
    for h in range(heads):
        scores = dot(proj[0, :, at[h]], proj[1, :, at[h]], 1, 1) * SCALE
        shifted = jnp.exp(scores - jnp.max(scores, axis=-1, keepdims=True))
        soft = shifted / jnp.sum(shifted, axis=-1, keepdims=True)
        softs[h] = soft
        alld[side, chunk_of(3, h), :, within[h]] = dot(
            soft.astype(BF), proj[2, :, at[h]], 1, 0
        ).astype(BF)
        if h % 4 == 3:
            share_chunk(chunk_of(3, h))
    weights[3].wait()
    part_out[...] = dot(alld[side, 0], wo[:256, :], 1, 0) + dot(alld[side, 1], wo[256:, :], 1, 0)
    theirs = pl.ds(pl.multiple_of((1 - core) * 128, 128), 128)
    ours = pl.ds(pl.multiple_of(core * 128, 128), 128)
    swap_out = partner(part_out.at[theirs, :], oland, 2)
    swap_out.start()
    wait(forward_g)
    share_feature(1, g[...].astype(F32).T.astype(BF))
    proj[3] = dot(g[...], wo[...], 1, 1).astype(BF)

    def send_back(k, src, dst, j):
        landing = pl.ds(pl.multiple_of((mine // 2) * BLOCK, BLOCK), BLOCK)
        return pltpu.make_async_remote_copy(
            src_ref=src.at[j * BLOCK : (j + 1) * BLOCK, :],
            dst_ref=dst.at[landing, :],
            send_sem=bsend.at[k, j],
            recv_sem=brecv.at[k, mine // 2],
            device_id=device(base, core * 8 + j),
            device_id_type=MESH,
        )

    def deliver(k, src, dst):
        for j in range(8):

            @pl.when(core * 8 + j != mine)
            def _():
                send_back(k, src, dst, j).start()

            @pl.when(core * 8 + j == mine)
            def _():
                dst[own_class, :] = src[j * BLOCK : (j + 1) * BLOCK, :]

    wait(swap_out)
    oret[...] = (part_out[ours, :] + oland[...]).astype(BF)
    deliver(0, oret, oin)

    def backward(h):
        q, k, v, do = (proj[i, :, at[h]] for i in range(4))
        soft = softs[h]
        d_soft = dot(do, v, 1, 1)
        d_scores = soft * (d_soft - jnp.sum(soft * d_soft, axis=-1, keepdims=True))
        d_scaled = (d_scores * SCALE).astype(BF)
        w = within[h]
        alld[side, chunk_of(0, h), :, w] = dot(d_scaled, k, 1, 0).astype(BF)
        alld[side, chunk_of(1, h), :, w] = dot(d_scaled, q, 0, 0).astype(BF)
        alld[side, chunk_of(2, h), :, w] = dot(soft.astype(BF), do, 0, 0).astype(BF)
        if h % 4 == 3:
            for i in range(3):
                share_chunk(chunk_of(i, h))

    def line(way, t, c):
        return pltpu.make_async_remote_copy(
            src_ref=outbox.at[way, t, c],
            dst_ref=inbox.at[way, t, c],
            send_sem=zsend.at[way, t, c],
            recv_sem=zrecv.at[way, t, c],
            device_id={"chip": lax.rem(chip + (low if way == 0 else low * (high - 1)), low * high)},
            device_id_type=MESH,
        )

    def term(c):
        kind = jnp.where(c < 2, 1, 0)
        total = None
        for j in range(1, low):
            side_chunk(c, j).wait_recv()
        for s in range(low):
            part = dot(allf[kind, s].reshape(high * rows, 256), alld[s, c], 1, 0)
            total = part if total is None else total + part
        terms[c] = total.reshape(high, rows, 256)

    def relay(way, c):
        for t in range(high - 1, 0, -1) if way == 0 else range(high - 1):
            ahead = level < t if way == 0 else level > t
            first = level == (0 if way == 0 else high - 1)

            @pl.when(ahead & first)
            def _():
                outbox[way, t, c] = terms[c, t].astype(BF)
                line(way, t, c).start()

            @pl.when(ahead & jnp.logical_not(first))
            def _():
                line(way, t, c).wait_recv()
                outbox[way, t, c] = (terms[c, t] + inbox[way, t, c].astype(F32)).astype(BF)
                line(way, t, c).start()

    chunks = 8

    def step(s, fresh):
        if fresh:
            term(s)
        for way, lag in ((0, level), (1, high - 1 - level)):
            c = s - lag

            @pl.when((c >= 0) & (c < chunks))
            def _():
                relay(way, c)

    for h in range(4):
        backward(h)
    for k in range(2):
        for j in range(1, low):
            side_feature(k, j).wait_recv()
    step(0, True)
    for h in range(4, 8):
        backward(h)
    step(1, True)
    total = None
    for i in range(3):
        for half in range(2):
            part = dot(alld[side, 2 + 3 * half + i], wi[i, :, half * 256 : (half + 1) * 256], 1, 1)
            total = part if total is None else total + part
    part_dn[...] = total
    swap_dn = partner(part_dn.at[theirs, :], dland, 3)
    swap_dn.start()
    step(2, True)
    wait(swap_dn)
    standard, inverse = normalise(x[ours, :])
    weighted = (part_dn[ours, :] + dland[...]) * gain[...]
    mean_one = jnp.mean(weighted, axis=-1, keepdims=True)
    mean_two = jnp.mean(weighted * standard, axis=-1, keepdims=True)
    dret[...] = (inverse * (weighted - mean_one - standard * mean_two)).astype(BF)
    deliver(1, dret, din)

    def fresh_step(s, _):
        step(s, True)
        return 0

    def late_step(s, _):
        step(s, False)
        return 0

    lax.fori_loop(3, chunks, fresh_step, 0)
    lax.fori_loop(chunks, chunks + high - 1, late_step, 0)

    home = mine // 8
    inverse_perm = permutation(True)
    for k, (src, dst, result) in enumerate(((oret, oin, out), (dret, din, grad))):
        for j in range(8):

            @pl.when(core * 8 + j != mine)
            def _():
                send_back(k, src, dst, j).wait_send()

            @pl.when(j * 2 + home != mine)
            def _():
                pltpu.make_async_remote_copy(
                    src_ref=src.at[j * BLOCK : (j + 1) * BLOCK, :],
                    dst_ref=dst.at[j * BLOCK : (j + 1) * BLOCK, :],
                    send_sem=bsend.at[k, j],
                    recv_sem=brecv.at[k, j],
                    device_id={"core": 1 - core},
                    device_id_type=MESH,
                ).wait_recv()

        result[...] = jnp.dot(inverse_perm, dst[...], preferred_element_type=F32).astype(BF)

    w_rows = pl.ds(pl.multiple_of(chip * rows, rows), rows)
    gain_sum = jnp.zeros((rows, 1), F32)
    for c in range(chunks):
        span = slice(c * 256, (c + 1) * 256)
        fin[:, span] = terms[c, level]
        for way, there in ((0, level > 0), (1, level < high - 1)):

            @pl.when(there)
            def _():
                line(way, level, c).wait_recv()
                fin[:, span] += inbox[way, level, c].astype(F32)

        if c >= 2:
            half, i = divmod(c - 2, 3)
            w = wi[i, w_rows, half * 256 : (half + 1) * 256].astype(F32)
            gain_sum = gain_sum + jnp.sum(w * fin[:, span], axis=-1, keepdims=True)
    lane = lax.broadcasted_iota(jnp.int32, (rows, D), 1)
    mine_lane = chip * rows + lax.broadcasted_iota(jnp.int32, (rows, D), 0)
    my_gain = jnp.sum(jnp.where(lane == mine_lane, gain[...], 0.0), axis=-1, keepdims=True)
    fin[:, chunks * 256 :] = jnp.broadcast_to(gain_sum / my_gain, (rows, 128))
    few = rows // 2
    their_rows = pl.ds(pl.multiple_of((1 - core) * few, few), few)
    our_rows = pl.ds(pl.multiple_of(core * few, few), few)
    swap_fin = partner(fin.at[their_rows, :], fland, 4)
    swap_fin.start()

    def place_rows(who, values):
        for c in range(chunks):
            piece = values(slice(c * 256, (c + 1) * 256))
            if c < 2:
                gout[:, pl.ds(pl.multiple_of(who * HALF + c * 256, 256), 256)] = piece
            else:
                half, i = divmod(c - 2, 3)
                where = pl.ds(pl.multiple_of(i * D + who * HALF + half * 256, 256), 256)
                gin[:, where] = piece

    place_rows(core, lambda s: fin[our_rows, s])
    wait(swap_fin)
    place_rows(1 - core, lambda s: fland[:, s])
    gsum[...] = (fin[our_rows, chunks * 256 :] + fland[:, chunks * 256 :]).T[:1, :]

    for k in range(2):
        for j in range(1, low):
            side_feature(k, j).wait_send()

    def drain(c, _):
        for j in range(1, low):
            side_chunk(c, j).wait_send()
        for t in range(high):
            for way in range(2):
                sent = level < t if way == 0 else level > t

                @pl.when(sent)
                def _():
                    line(way, t, c).wait_send()

        return 0

    lax.fori_loop(0, chunks, drain, 0)


def settle_kernel(*refs):
    sem = refs[-1]
    half = (len(refs) - 1) // 2
    copies = [pltpu.make_async_copy(refs[i], refs[half + i], sem.at[i]) for i in range(half)]
    for c in copies:
        c.start()
    for c in copies:
        c.wait()


def settle(*arrays):
    anywhere = [pl.BlockSpec(memory_space=pl.ANY)] * len(arrays)
    held = [vmem()] * len(arrays)
    return pl.pallas_call(
        settle_kernel,
        out_shape=[jax.ShapeDtypeStruct(a.shape, a.dtype) for a in arrays],
        in_specs=held,
        out_specs=anywhere,
        scratch_shapes=[pltpu.SemaphoreType.DMA((len(arrays),))],
        compiler_params=pltpu.CompilerParams(vmem_limit_bytes=8 * MB),
    )(*arrays)


def per_device(tokens, norm_gain, in_projection, out_projection, out_cotangent):
    chips = lax.axis_size("chip")
    low = 1
    while 4 * low * low <= chips:
        low *= 2
    high = chips // low
    rows = D // chips
    few = rows // 2
    sems = pltpu.SemaphoreType.DMA
    layer_output, grad_tokens, grad_in, grad_out, gain_sum = pl.pallas_call(
        functools.partial(kernel, low, high),
        out_shape=[
            jax.ShapeDtypeStruct((128, D), BF),
            jax.ShapeDtypeStruct((128, D), BF),
            jax.ShapeDtypeStruct((few, 3 * D), F32),
            jax.ShapeDtypeStruct((few, D), F32),
            jax.ShapeDtypeStruct((1, few), F32),
        ],
        in_specs=[vmem()] * 3 + [pl.BlockSpec(memory_space=pl.ANY)] * 2,
        out_specs=[vmem()] * 5,
        scratch_shapes=[
            pltpu.VMEM((128, D), BF),
            pltpu.VMEM((128, D), BF),
            pltpu.VMEM((256, D), BF),
            pltpu.VMEM((256, D), BF),
            pltpu.VMEM((3, D, HALF), BF),
            pltpu.VMEM((HALF, D), BF),
            pltpu.VMEM((256, D), BF),
            pltpu.VMEM((4, 256, HALF), BF),
            pltpu.VMEM((8, 256, 256), F32),
            pltpu.VMEM((2, high, low, rows, 256), BF),
            pltpu.VMEM((2, low, high, rows, 256), BF),
            pltpu.VMEM((low, 8, 256, 256), BF),
            pltpu.VMEM((8, high, rows, 256), F32),
            pltpu.VMEM((2, high, 8, rows, 256), BF),
            pltpu.VMEM((2, high, 8, rows, 256), BF),
            pltpu.VMEM((256, D), F32),
            pltpu.VMEM((256, D), F32),
            pltpu.VMEM((128, D), F32),
            pltpu.VMEM((128, D), F32),
            pltpu.VMEM((128, D), BF),
            pltpu.VMEM((128, D), BF),
            pltpu.VMEM((128, D), BF),
            pltpu.VMEM((128, D), BF),
            pltpu.VMEM((rows, 8 * 256 + 128), F32),
            pltpu.VMEM((few, 8 * 256 + 128), F32),
            sems((4,)),
            sems((2, GROUP)),
            sems((2, GROUP)),
            sems((5,)),
            sems((5,)),
            sems((2, low)),
            sems((2, low)),
            sems((8, low)),
            sems((8, low)),
            sems((2, high, 8)),
            sems((2, high, 8)),
            sems((2, 8)),
            sems((2, 8)),
        ],
        compiler_params=pltpu.CompilerParams(
            collective_id=0, has_side_effects=True, vmem_limit_bytes=56 * MB
        ),
    )(tokens, out_cotangent, norm_gain.reshape(1, D), in_projection, out_projection)
    settled = settle(layer_output, grad_tokens, grad_in, grad_out, gain_sum)
    return settled[0], settled[1], settled[2], settled[3].T, settled[4].reshape(few)


def solution(mesh):
    parts, bricks = mesh.devices.shape
    fine = Mesh(mesh.devices.reshape(parts, bricks // 2, 2), ("parts", "chip", "core"))
    every = ("parts", "chip", "core")
    placed = (P(every, None), P(), P(), P(), P(every, None))
    return jax.shard_map(
        per_device,
        mesh=fine,
        in_specs=placed,
        out_specs=(
            P(every, None),
            P(every, None),
            P(every, None),
            P("parts", ("chip", "core")),
            P(every),
        ),
        check_vma=False,
    )
```
